32 devices in a mesh: narrow: 4 (over z), wide: 8 (over y, x, core).
Axes of the slice: x: 2, y: 2, z: 4, core: 2. Of those that a mesh axis runs over, the one named last changes fastest.
Arguments:
- tokens: bfloat16 [16384, 1024], P('wide', 'narrow'), may hold values from -6 to 6
- condition: bfloat16 [16, 1024], P('wide'), may hold values from -6 to 6
- w_ada: bfloat16 [1024, 6, 1024], P('wide', None, 'narrow'), may hold values from -0.1875 to 0.1875
- b_ada: bfloat16 [6, 1024], P(None, ('narrow', 'wide')), may hold values from -3 to 3
- w_qkv: bfloat16 [1024, 3, 1024], P('wide', None, 'narrow'), may hold values from -0.1875 to 0.1875
- b_qv: bfloat16 [2, 1024], P(None, ('narrow', 'wide')), may hold values from -1.1953125 to 1.1953125
- w_proj: bfloat16 [1024, 1024], P('narrow', 'wide'), may hold values from -0.75 to 0.75
- b_proj: bfloat16 [1024], P(('narrow', 'wide')), may hold values from -3 to 3
- w_fc1: bfloat16 [1024, 4096], P('wide', 'narrow'), may hold values from -0.1875 to 0.1875
- b_fc1: bfloat16 [4096], P(('narrow', 'wide')), may hold values from -3 to 3
- w_fc2: bfloat16 [4096, 1024], P('narrow', 'wide'), may hold values from -0.09375 to 0.09375
- b_fc2: bfloat16 [1024], P(('narrow', 'wide')), may hold values from -3 to 3
- cotangent: bfloat16 [16384, 1024], P('wide', 'narrow'), may hold values from -6 to 6
Outputs:
- output: bfloat16 [16384, 1024], P('wide', 'narrow')
- grad_tokens: float32 [16384, 1024], P('wide', 'narrow')
- grad_cond: float32 [16, 1024], P('wide')
- grad_w_ada: float32 [1024, 6, 1024], P('wide', None, 'narrow')
- grad_b_ada: float32 [6, 1024], P(None, ('narrow', 'wide'))
- grad_w_qkv: float32 [1024, 3, 1024], P('wide', None, 'narrow')
- grad_b_qv: float32 [2, 1024], P(None, ('narrow', 'wide'))
- grad_w_proj: float32 [1024, 1024], P('narrow', 'wide')
- grad_b_proj: float32 [1024], P(('narrow', 'wide'))
- grad_w_fc1: float32 [1024, 4096], P('wide', 'narrow')
- grad_b_fc1: float32 [4096], P(('narrow', 'wide'))
- grad_w_fc2: float32 [4096, 1024], P('narrow', 'wide')
- grad_b_fc2: float32 [1024], P(('narrow', 'wide'))
The draws below stay inside these ranges and needn't reach their ends.
All inputs are finite; a program needn't handle non-finite values.
Results may differ from the reference program's by a relative error of at most 0.019.
The reference program's roundings to bfloat16 on the way count: a program that leaves them out, or rounds other values in their place, can miss the bound.
Values may be sent and summed in bfloat16 or wider, within the bound.
A program may use at most 128 MiB of HBM per device.

```python
import jax
import jax.numpy as jnp
from jax import lax

D = 1024
HEADS = 16
FF = 4096
LENGTH = 1024
HEAD_DIM = 64
SEQS = 16
TOKENS = 16384
N_NARROW = 4


def block_levels(key, extent, split, least, largest):
    loudness = 1.0
    for dim, shards_of in split:
        steps = jax.random.uniform(jax.random.fold_in(jax.random.fold_in(key, 6), dim), (shards_of,), jnp.float32, least / len(split), largest / len(split))
        loudness = loudness * jnp.repeat(jnp.exp(steps), extent[dim] // shards_of).reshape((-1,) + (1,) * (len(extent) - 1 - dim))
    return loudness


def gaussian(stream_key, shape, spread, most, pieces=(), held_as=jnp.bfloat16):
    array = jax.random.normal(stream_key, shape, jnp.float32) * spread
    if len(pieces) > 0:
        array = block_levels(stream_key, shape, pieces, -0.22, 0.18) * array
    return jnp.clip(array, min=-most, max=most).astype(held_as)


def setup_inputs(seed: int = 0) -> dict:
    splits = jax.random.split(jax.random.key(seed), 14)
    return {
        "tokens": gaussian(splits[0], (TOKENS, D), 1.0, 6.0, ((0, 8), (1, 4))),
        "condition": gaussian(splits[1], (SEQS, D), 1.0, 6.0, ((0, 8),)),
        "w_ada": gaussian(splits[2], (D, 6, D), D ** -0.5, 0.1875, ((0, 8), (2, 4))),
        "b_ada": gaussian(splits[3], (6, D), 0.5, 3.0, ((1, 32),)),
        "w_qkv": gaussian(splits[4], (D, 3, D), D ** -0.5, 0.1875, ((0, 8), (2, 4))),
        "b_qv": gaussian(splits[5], (2, D), 0.2, 1.1953125, ((1, 32),)),
        "w_proj": gaussian(splits[6], (D, D), (D // 16) ** -0.5, 0.75, ((0, 4), (1, 8))),
        "b_proj": gaussian(splits[7], (D,), 0.5, 3.0, ((0, 32),)),
        "w_fc1": gaussian(splits[8], (D, FF), D ** -0.5, 0.1875, ((0, 8), (1, 4))),
        "b_fc1": gaussian(splits[9], (FF,), 0.5, 3.0, ((0, 32),)),
        "w_fc2": gaussian(splits[10], (FF, D), FF ** -0.5, 0.09375, ((0, 4), (1, 8))),
        "b_fc2": gaussian(splits[11], (D,), 0.5, 3.0, ((0, 32),)),
        "cotangent": gaussian(splits[12], (TOKENS, D), 1.0, 6.0, ((0, 8), (1, 4))),
    }


norm_epsilon = 1e-06
gelu_factor = 0.7978845608028654
gelu_cubic = 0.044715

@jax.custom_vjp
def low(v):
    return lax.optimization_barrier(v.astype(jnp.bfloat16)).astype(jnp.float32)

@jax.custom_vjp
def low_back(v):
    return v

def low_keep(v):
    return (low(v), None)

def low_pass(kept, grad):
    return (grad,)

def back_keep(v):
    return (v, None)

def back_low(kept, grad):
    return (low(grad),)
low.defvjp(low_keep, low_pass)
low_back.defvjp(back_keep, back_low)

def layer_norm(values):
    row_mean = lax.optimization_barrier(jnp.mean(values, axis=-1, keepdims=True))
    centered = values - row_mean
    row_var = lax.optimization_barrier(jnp.mean(centered * centered, axis=-1, keepdims=True))
    return centered * lax.rsqrt(row_var + norm_epsilon)

def gelu_tanh(values):
    return 0.5 * values * (1.0 + jnp.tanh(gelu_factor * (values + gelu_cubic * values * values * values)))

def product(left_side, right_side):
    return jnp.dot(left_side, right_side, precision=lax.Precision.HIGHEST)

def split_sum(left_side, right_side):
    block_size = left_side.shape[1] // N_NARROW
    running = jnp.zeros((left_side.shape[0], right_side.shape[1]), left_side.dtype)
    for block_index in range(N_NARROW):
        offset = block_index * block_size
        running = running + low(product(left_side[:, offset:offset + block_size], right_side[offset:offset + block_size]))
    return running

def one_sequence(params, seq_tokens, seq_cond):
    w_ada, b_ada, w_qkv, b_qv, w_proj, b_proj, w_fc1, b_fc1, w_fc2, b_fc2 = params
    cond_act = low(jax.nn.silu(seq_cond))
    modulation = low_back(product(cond_act[None, :], w_ada.reshape(D, 6 * D))[0] + b_ada.reshape(6 * D)).reshape(6, D)
    hidden_one = low(layer_norm(seq_tokens) * (1.0 + modulation[1]) + modulation[0])
    qkv_bias = jnp.stack([b_qv[0], jnp.zeros_like(b_qv[0]), b_qv[1]])
    qkv = low_back(low(product(hidden_one, w_qkv.reshape(D, 3 * D)).reshape(LENGTH, 3, D) + qkv_bias))
    query_rows = qkv[:, 0].reshape(LENGTH, HEADS, HEAD_DIM)
    key_rows = qkv[:, 1].reshape(LENGTH, HEADS, HEAD_DIM)
    value_rows = qkv[:, 2].reshape(LENGTH, HEADS, HEAD_DIM)
    scores = low_back(jnp.einsum('qhd,khd->hqk', query_rows, key_rows, precision=lax.Precision.HIGHEST) * HEAD_DIM ** (-0.5))
    soft_weights = low(jax.nn.softmax(scores, axis=-1))
    attended = jnp.einsum('hqk,khd->qhd', soft_weights, value_rows, precision=lax.Precision.HIGHEST).reshape(LENGTH, D)
    attended = low_back(low(attended))
    attn_branch = low_back(split_sum(attended, w_proj) + b_proj)
    residual = seq_tokens + modulation[2] * attn_branch
    hidden_two = low(layer_norm(residual) * (1.0 + modulation[4]) + modulation[3])
    pre_act = low_back(product(hidden_two, w_fc1) + b_fc1)
    activated = low(gelu_tanh(pre_act))
    mlp_branch = low_back(split_sum(activated, w_fc2) + b_fc2)
    return residual + modulation[5] * mlp_branch

def reference(tokens, condition, w_ada, b_ada, w_qkv, b_qv, w_proj, b_proj, w_fc1, b_fc1, w_fc2, b_fc2, cotangent):
    params = (w_ada.astype(jnp.float32), b_ada.astype(jnp.float32), w_qkv.astype(jnp.float32), b_qv.astype(jnp.float32), w_proj.astype(jnp.float32), b_proj.astype(jnp.float32), w_fc1.astype(jnp.float32), b_fc1.astype(jnp.float32), w_fc2.astype(jnp.float32), b_fc2.astype(jnp.float32))
    seq_inputs = tokens.astype(jnp.float32).reshape(SEQS, LENGTH, D)
    cond_inputs = condition.astype(jnp.float32)

    def forward(seq_values, cond_values, weights):

        def per_sequence(element):
            return one_sequence(weights, element[0], element[1])
        return lax.map(jax.checkpoint(per_sequence), (seq_values, cond_values))
    outputs, pullback = jax.vjp(forward, seq_inputs, cond_inputs, params)
    grad_inputs, grad_cond, grad_params = pullback(cotangent.astype(jnp.float32).reshape(SEQS, LENGTH, D))
    return (outputs.reshape(TOKENS, D).astype(jnp.bfloat16), grad_inputs.reshape(TOKENS, D), grad_cond, grad_params[0], grad_params[1], grad_params[2], grad_params[3], grad_params[4], grad_params[5], grad_params[6], grad_params[7], grad_params[8], grad_params[9])
```

```python
import jax
import jax.numpy as jnp
from jax import lax
from jax.sharding import Mesh
from jax.sharding import PartitionSpec as P

HEADS = 16


norm_epsilon = 1e-06
gelu_factor = 0.7978845608028654
gelu_cubic = 0.044715


def gelu_tanh(values):
    return (
        0.5
        * values
        * (1.0 + jnp.tanh(gelu_factor * (values + gelu_cubic * values * values * values)))
    )


def gelu_slope(values):
    inner = jnp.tanh(gelu_factor * (values + gelu_cubic * values * values * values))
    return 0.5 * (1.0 + inner) + 0.5 * values * (1.0 - inner * inner) * gelu_factor * (
        1.0 + 3.0 * gelu_cubic * values * values
    )


def norm_forward(values):
    row_mean = jnp.mean(values, axis=1, keepdims=True)
    row_var = jnp.mean(values * values, axis=1, keepdims=True) - row_mean * row_mean
    inverse = lax.rsqrt(row_var + norm_epsilon)
    return (values - row_mean) * inverse, inverse


def norm_backward(grad_normed, normed, inverse):
    mean_one = jnp.mean(grad_normed, axis=1, keepdims=True)
    mean_two = jnp.mean(grad_normed * normed, axis=1, keepdims=True)
    return inverse * (grad_normed - mean_one - normed * mean_two)


def swap_core(values):
    return lax.ppermute(values, "core", [(0, 1), (1, 0)])


def pair_gather(rows):
    other = swap_core(rows)
    mine_first = lax.axis_index("core") == 0
    return jnp.concatenate(
        [jnp.where(mine_first, rows, other), jnp.where(mine_first, other, rows)], axis=0
    )


def pair_scatter(partial):
    half = partial.shape[0] // 2
    core = lax.axis_index("core")
    sent = lax.dynamic_slice_in_dim(partial, (1 - core) * half, half, 0)
    kept = lax.dynamic_slice_in_dim(partial, core * half, half, 0)
    return kept.astype(jnp.float32) + swap_core(sent).astype(jnp.float32)


def shift_narrow(values, step):
    size = lax.axis_size("narrow")
    return lax.ppermute(values, "narrow", [(i, (i + step) % size) for i in range(size)])


def flip_col(values, bit):
    size = lax.axis_size("col")
    return lax.ppermute(values, "col", [(i, i ^ bit) for i in range(size)])


def col_bits():
    bits = []
    bit = 1
    while bit < lax.axis_size("col"):
        bits.append(bit)
        bit *= 2
    return bits


def gather_chips(shard):
    half = shard.shape[0] // 2
    up = shift_narrow(shard, 1)
    down = shift_narrow(shard, -1)
    far = jnp.concatenate([shift_narrow(up[:half], 1), shift_narrow(down[half:], -1)], axis=0)
    line = jnp.stack([shard, up, far, down])
    bits = col_bits()
    sides = []
    for part, order in ((line[:, :half], bits), (line[:, half:], bits[::-1])):
        pieces = {0: part}
        for bit in order:
            for mask in list(pieces):
                pieces[mask | bit] = flip_col(pieces[mask], bit)
        sides.append(jnp.stack([pieces[mask] for mask in range(len(pieces))]))
    return sides


def arrange(sides, low, high):
    col = lax.axis_index("col")
    count = lax.axis_size("col")
    blocks = []
    for side in sides:
        cut = side[..., low:high]
        blocks.append(
            jnp.stack(
                [lax.dynamic_index_in_dim(cut, c ^ col, 0, keepdims=False) for c in range(count)],
                axis=1,
            )
        )
    return jnp.concatenate(blocks, axis=2)


def add_low(left, right):
    return (left.astype(jnp.float32) + right.astype(jnp.float32)).astype(jnp.bfloat16)


def scatter_chips(blocks):
    col = lax.axis_index("col")
    count = lax.axis_size("col")
    half = blocks.shape[2] // 2
    bits = col_bits()
    halves = []
    for part, order in ((blocks[:, :, :half], bits), (blocks[:, :, half:], bits[::-1])):
        pieces = {
            mask: lax.dynamic_index_in_dim(part, mask ^ col, 1, keepdims=False)
            for mask in range(count)
        }
        for bit in order:
            for mask in [m for m in pieces if not m & bit]:
                pieces[mask] = add_low(pieces[mask], flip_col(pieces.pop(mask | bit), bit))
        halves.append(pieces[0])
    line = jnp.concatenate(halves, axis=1)
    own, up, far, down = line[0], line[1], line[2], line[3]
    up_low = add_low(up[:half], shift_narrow(far[:half], -1))
    down_high = add_low(down[half:], shift_narrow(far[half:], 1))
    up_all = jnp.concatenate([up_low, up[half:]], axis=0)
    down_all = jnp.concatenate([down[:half], down_high], axis=0)
    return (
        own.astype(jnp.float32)
        + shift_narrow(up_all, -1).astype(jnp.float32)
        + shift_narrow(down_all, 1).astype(jnp.float32)
    )


def core_rows(values, split_axis, concat_axis):
    return lax.all_to_all(values, "core", split_axis, concat_axis, tiled=True)


def to_images(values, seq_count, half):
    width = values.shape[1]
    shaped = core_rows(values.reshape(seq_count, 2, half, width), 1, 0)
    return lax.all_to_all(
        shaped.reshape(2 * seq_count, half, width), "narrow", 0, 2, tiled=True
    ).reshape(half, -1)


def from_images(values, seq_count):
    half = values.shape[0]
    shaped = lax.all_to_all(values[None], "narrow", 2, 0, tiled=True)
    return core_rows(shaped[:, None], 0, 1).reshape(seq_count * 2 * half, -1)


def per_device(
    tokens,
    condition,
    w_ada,
    b_ada,
    w_qkv,
    b_qv,
    w_proj,
    b_proj,
    w_fc1,
    b_fc1,
    w_fc2,
    b_fc2,
    cotangent,
):
    seq_count = condition.shape[0]
    length = tokens.shape[0] // seq_count
    half = length // 2
    feature_count = condition.shape[1]
    head_dim = feature_count // HEADS
    score_scale = head_dim ** (-0.5)
    narrow = lax.axis_index("narrow")
    col = lax.axis_index("col")
    core = lax.axis_index("core")
    n_size = lax.axis_size("narrow")
    w_size = 2 * lax.axis_size("col")
    wide = 2 * col + core
    part_width = feature_count // 2
    head_count = part_width // head_dim
    unit = feature_count // n_size
    pair = unit // 2
    fc_unit = w_fc1.shape[1]
    fc_half = fc_unit // 2
    rows_low = w_fc1.shape[0]
    rows = 2 * rows_low

    def attend(seq_block):
        outputs = []
        lse_list = []
        for head_index in range(head_count):
            offset = head_index * head_dim
            query_rows = seq_block[0][:, offset : offset + head_dim]
            key_rows = seq_block[1][:, offset : offset + head_dim]
            value_rows = seq_block[2][:, offset : offset + head_dim]
            scores = (
                jnp.einsum("qd,kd->qk", query_rows, key_rows, preferred_element_type=jnp.float32)
                * score_scale
            )
            row_top = jnp.max(scores, axis=1, keepdims=True)
            raised = jnp.exp(scores - row_top)
            row_total = jnp.sum(raised, axis=1, keepdims=True)
            soft_weights = (raised / row_total).astype(jnp.bfloat16)
            outputs.append(jnp.dot(soft_weights, value_rows, preferred_element_type=jnp.float32))
            lse_list.append(row_top[:, 0] + jnp.log(row_total[:, 0]))
        return (jnp.concatenate(outputs, axis=1), jnp.stack(lse_list))

    def attend_back(packed):
        seq_block, lse_rows, grad_block = packed
        pieces = []
        for head_index in range(head_count):
            offset = head_index * head_dim
            query_rows = seq_block[0][:, offset : offset + head_dim]
            key_rows = seq_block[1][:, offset : offset + head_dim]
            value_rows = seq_block[2][:, offset : offset + head_dim]
            grad_head = grad_block[:, offset : offset + head_dim]
            scores = (
                jnp.einsum("qd,kd->qk", query_rows, key_rows, preferred_element_type=jnp.float32)
                * score_scale
            )
            soft_float = jnp.exp(scores - lse_rows[head_index][:, None])
            soft_weights = soft_float.astype(jnp.bfloat16)
            grad_value = jnp.einsum(
                "qk,qd->kd", soft_weights, grad_head, preferred_element_type=jnp.float32
            )
            grad_soft = jnp.einsum(
                "qd,kd->qk", grad_head, value_rows, preferred_element_type=jnp.float32
            )
            inner = jnp.sum(soft_float * grad_soft, axis=1, keepdims=True)
            grad_scores = (soft_float * (grad_soft - inner)).astype(jnp.bfloat16)
            grad_query = (
                jnp.dot(grad_scores, key_rows, preferred_element_type=jnp.float32) * score_scale
            )
            grad_key = (
                jnp.einsum("qk,qd->kd", grad_scores, query_rows, preferred_element_type=jnp.float32)
                * score_scale
            )
            pieces.append([grad_query, grad_key, grad_value])
        return jnp.concatenate(
            [piece[c] for c in range(3) for piece in pieces], axis=1
        ).astype(jnp.bfloat16)


    def turned(values, axis):
        return jnp.take(values, (narrow - jnp.arange(n_size)) % n_size, axis=axis)

    qkv_cut = core_rows(jnp.transpose(w_qkv, (1, 0, 2)), 2, 1)
    proj_cut = core_rows(w_proj, 0, 1).T
    fc1_cut = core_rows(w_fc1, 1, 0)
    fc2_cut = core_rows(w_fc2, 0, 1).T
    pack_one = jnp.concatenate([qkv_cut[0], qkv_cut[1], qkv_cut[2], proj_cut], axis=1)
    sides_one = gather_chips(pack_one)
    pack_two = jnp.concatenate([fc1_cut, fc2_cut], axis=1)
    sides_two = gather_chips(pack_two)

    def matrix(sides, low, high):
        blocks = arrange(sides, low, high)
        return jnp.transpose(blocks, (1, 2, 0, 3)).reshape(feature_count, -1)

    qkv_mats = [matrix(sides_one, c * pair, (c + 1) * pair) for c in range(3)]
    qkv_full = jnp.concatenate(qkv_mats, axis=1)
    proj_full = matrix(sides_one, 3 * pair, 4 * pair)
    fc1_full = matrix(sides_two, 0, fc_half)
    fc2_full = matrix(sides_two, fc_half, 2 * fc_half)

    inputs = to_images(tokens, seq_count, half).astype(jnp.float32)
    small = jnp.concatenate(
        [
            b_ada.reshape(-1),
            b_qv.reshape(-1),
            b_proj,
            b_fc2,
            b_fc1,
            condition.reshape(-1),
        ]
    )
    smalls = lax.all_gather(small, ("narrow", "col", "core"))
    part = b_proj.shape[0]

    def full_bias(low, count):
        return jnp.transpose(
            smalls[:, low : low + count * part].reshape(n_size * w_size, count, part), (1, 0, 2)
        ).reshape(count, feature_count)

    ada_bias = full_bias(0, 6).astype(jnp.float32)
    qv_bias = full_bias(6 * part, 2)
    proj_bias = full_bias(8 * part, 1).astype(jnp.float32)
    fc2_bias = full_bias(9 * part, 1).astype(jnp.float32)
    fc1_size = b_fc1.shape[0]
    fc1_rows = smalls[:, 10 * part : 10 * part + fc1_size].reshape(n_size, 2, fc_half)
    fc1_bias = turned(lax.dynamic_index_in_dim(fc1_rows, core, 1, keepdims=False), 0)
    fc1_bias = fc1_bias.reshape(1, -1).astype(jnp.float32)
    qv_rows = lax.dynamic_index_in_dim(
        qv_bias.reshape(2, n_size, 2, pair), core, 2, keepdims=False
    )
    qv_rows = turned(qv_rows, 1).reshape(2, -1).astype(jnp.float32)
    qkv_bias = jnp.concatenate([qv_rows[0], jnp.zeros_like(qv_rows[0]), qv_rows[1]])

    cond_all = smalls[:w_size, 10 * part + fc1_size :].reshape(-1, feature_count)
    cond_act_all = jax.nn.silu(cond_all.astype(jnp.float32)).astype(jnp.bfloat16)
    cond_cols = lax.dynamic_slice_in_dim(cond_act_all, wide * rows_low, rows_low, 1)
    mod_part = jnp.einsum("sd,dcn->scn", cond_cols, w_ada, preferred_element_type=jnp.float32)
    mod_total = lax.psum(mod_part, ("col", "core"))
    mod_rows = lax.dynamic_slice_in_dim(mod_total, col * n_size, n_size, 0)
    modulation = lax.all_to_all(mod_rows, "narrow", 0, 2, tiled=True).reshape(6, -1) + ada_bias
    shift_one, scale_one, gate_one, shift_two, scale_two, gate_two = [
        modulation[i : i + 1] for i in range(6)
    ]

    normed_one, inverse_one = norm_forward(inputs)
    hidden_one = (normed_one * (1.0 + scale_one) + shift_one).astype(jnp.bfloat16)
    hidden_one_full = pair_gather(hidden_one)
    qkv_low = (
        jnp.dot(hidden_one_full, qkv_full, preferred_element_type=jnp.float32) + qkv_bias
    ).astype(jnp.bfloat16)
    qkv_parts = [qkv_low[:, c * part_width : (c + 1) * part_width] for c in range(3)]
    attended, lse_rows = attend(qkv_parts)
    attended_low = attended.astype(jnp.bfloat16)
    attn_branch = (
        pair_scatter(
            jnp.einsum(
                "th,dh->td", attended_low, proj_full, preferred_element_type=jnp.float32
            ).astype(jnp.bfloat16)
        )
        + proj_bias
    )
    residual = inputs + attn_branch * gate_one
    normed_two, inverse_two = norm_forward(residual)
    hidden_two = (normed_two * (1.0 + scale_two) + shift_two).astype(jnp.bfloat16)
    hidden_two_full = pair_gather(hidden_two)
    grad_out = to_images(cotangent, seq_count, half).astype(jnp.float32)
    grad_mlp = (grad_out * gate_two).astype(jnp.bfloat16)
    grad_mlp_full = pair_gather(grad_mlp)
    pre_act = jnp.dot(hidden_two_full, fc1_full, preferred_element_type=jnp.float32) + fc1_bias
    activated = gelu_tanh(pre_act).astype(jnp.bfloat16)
    grad_act = jnp.dot(grad_mlp_full, fc2_full, preferred_element_type=jnp.float32)
    grad_pre = (grad_act * gelu_slope(pre_act)).astype(jnp.bfloat16)

    def blocked(grad):
        return jnp.transpose(
            grad.astype(jnp.bfloat16).reshape(-1, rows, n_size, grad.shape[1] // n_size),
            (2, 0, 1, 3),
        )

    grad_fc1_part = jnp.einsum(
        "td,tf->df", hidden_two_full, grad_pre, preferred_element_type=jnp.float32
    )
    grad_fc2_part = jnp.einsum(
        "td,tf->df", grad_mlp_full, activated, preferred_element_type=jnp.float32
    )
    total_fc1 = scatter_chips(blocked(grad_fc1_part))
    total_fc2 = scatter_chips(blocked(grad_fc2_part))
    grad_hidden_two = pair_scatter(
        jnp.einsum("tf,df->td", grad_pre, fc1_full, preferred_element_type=jnp.float32).astype(
            jnp.bfloat16
        )
    )
    mlp_branch = (
        pair_scatter(
            jnp.einsum(
                "tf,df->td", activated, fc2_full, preferred_element_type=jnp.float32
            ).astype(jnp.bfloat16)
        )
        + fc2_bias
    )
    output = from_images((residual + mlp_branch * gate_two).astype(jnp.bfloat16), seq_count)

    grad_residual = grad_out + norm_backward(
        grad_hidden_two * (1.0 + scale_two), normed_two, inverse_two
    )
    grad_attn = (grad_residual * gate_one).astype(jnp.bfloat16)
    grad_attn_full = pair_gather(grad_attn)
    grad_proj_part = jnp.einsum(
        "td,th->dh", grad_attn_full, attended_low, preferred_element_type=jnp.float32
    )
    grad_attended = jnp.dot(
        grad_attn_full, proj_full, preferred_element_type=jnp.float32
    ).astype(jnp.bfloat16)
    grad_qkv = attend_back((qkv_parts, lse_rows, grad_attended))
    grad_hidden_one = pair_scatter(
        jnp.einsum("tn,dn->td", grad_qkv, qkv_full, preferred_element_type=jnp.float32).astype(
            jnp.bfloat16
        )
    )
    grad_qkv_part = jnp.einsum(
        "td,tn->dn", hidden_one_full, grad_qkv, preferred_element_type=jnp.float32
    )
    grad_inputs = grad_residual + norm_backward(
        grad_hidden_one * (1.0 + scale_one), normed_one, inverse_one
    )
    grad_tokens = from_images(grad_inputs.astype(jnp.bfloat16), seq_count).astype(jnp.float32)
    total_one = scatter_chips(
        jnp.concatenate(
            [blocked(grad_qkv_part[:, c * part_width : (c + 1) * part_width]) for c in range(3)]
            + [blocked(grad_proj_part)],
            axis=3,
        )
    )

    def sums(values):
        return jnp.sum(values.astype(jnp.float32), axis=0)

    packed = jnp.concatenate(
        [
            sums(grad_hidden_one),
            sums(grad_hidden_one * normed_one),
            sums(grad_residual * attn_branch),
            sums(grad_hidden_two),
            sums(grad_hidden_two * normed_two),
            sums(grad_out * mlp_branch),
            sums(grad_mlp),
            sums(grad_attn),
            turned(sums(grad_pre).reshape(n_size, fc_half), 0).reshape(-1),
            turned(sums(grad_qkv[:, :part_width]).reshape(n_size, pair), 0).reshape(-1),
            turned(sums(grad_qkv[:, 2 * part_width :]).reshape(n_size, pair), 0).reshape(-1),
        ]
    )
    packs = lax.all_gather(packed, ("col", "narrow", "core"))
    packs = packs.reshape(-1, 2, packed.shape[0])
    d = feature_count
    grad_mod = jnp.sum(packs[:, :, : 6 * d], axis=1).astype(jnp.bfloat16).reshape(-1, 6, d)
    cores = jnp.sum(packs[:, :, 6 * d :], axis=0)
    both = jnp.sum(cores[:, : 2 * d], axis=0)
    place = narrow * w_size + wide
    grad_b_fc2 = lax.dynamic_slice_in_dim(both[:d], place * part, part, 0)
    grad_b_proj = lax.dynamic_slice_in_dim(both[d:], place * part, part, 0)
    fc1_sums = jnp.transpose(
        cores[:, 2 * d : 2 * d + n_size * fc_half].reshape(2, n_size, fc_half), (1, 0, 2)
    ).reshape(-1)
    grad_b_fc1 = lax.dynamic_slice_in_dim(fc1_sums, place * fc1_size, fc1_size, 0)
    qv_sums = jnp.transpose(
        cores[:, 2 * d + n_size * fc_half :].reshape(2, 2, n_size, pair), (1, 2, 0, 3)
    ).reshape(2, d)
    grad_b_qv = lax.dynamic_slice_in_dim(qv_sums, place * part, part, 1)
    ada_sums = jnp.sum(grad_mod.astype(jnp.float32), axis=0)
    grad_b_ada = lax.dynamic_slice_in_dim(ada_sums, place * part, part, 1)
    mod_slice = lax.dynamic_slice_in_dim(grad_mod, narrow * unit, unit, 2)
    grad_w_ada = jnp.einsum(
        "sd,scn->dcn", cond_cols, mod_slice, preferred_element_type=jnp.float32
    )
    cond_part = jnp.einsum("scn,dcn->sd", mod_slice, w_ada, preferred_element_type=jnp.float32)
    cond_parts = lax.all_gather(cond_part, ("narrow", "col", "core"))
    cond_rows = lax.dynamic_slice_in_dim(cond_parts, wide * seq_count, seq_count, 1)
    cond_sum = jnp.sum(cond_rows.reshape(n_size, w_size, seq_count, rows_low), axis=0)
    cond_total = jnp.transpose(cond_sum, (1, 0, 2)).reshape(seq_count, d)
    cond_float = condition.astype(jnp.float32)
    sigmoid_cond = jax.nn.sigmoid(cond_float)
    grad_cond = cond_total * sigmoid_cond * (1.0 + cond_float * (1.0 - sigmoid_cond))

    low_one = total_one.astype(jnp.bfloat16)
    qkv_out = jnp.stack([low_one[:, c * pair : (c + 1) * pair] for c in range(3)])
    grad_w_qkv = jnp.transpose(core_rows(qkv_out, 1, 2).astype(jnp.float32), (1, 0, 2))
    grad_w_proj = core_rows(low_one[:, 3 * pair :].T, 1, 0).astype(jnp.float32)
    grad_w_fc1 = core_rows(total_fc1.astype(jnp.bfloat16), 0, 1).astype(jnp.float32)
    grad_w_fc2 = core_rows(total_fc2.astype(jnp.bfloat16).T, 1, 0).astype(jnp.float32)
    return (
        output,
        grad_tokens,
        grad_cond,
        grad_w_ada,
        grad_b_ada,
        grad_w_qkv,
        grad_b_qv,
        grad_w_proj,
        grad_b_proj,
        grad_w_fc1,
        grad_b_fc1,
        grad_w_fc2,
        grad_b_fc2,
    )


W = ("col", "core")
NW = ("narrow", "col", "core")


def solution(mesh):
    devices = mesh.devices
    split = Mesh(devices.reshape(devices.shape[0], devices.shape[1] // 2, 2), NW)
    return jax.shard_map(
        per_device,
        mesh=split,
        in_specs=(
            P(W, "narrow"),
            P(W, None),
            P(W, None, "narrow"),
            P(None, NW),
            P(W, None, "narrow"),
            P(None, NW),
            P("narrow", W),
            P(NW),
            P(W, "narrow"),
            P(NW),
            P("narrow", W),
            P(NW),
            P(W, "narrow"),
        ),
        out_specs=(
            P(W, "narrow"),
            P(W, "narrow"),
            P(W, None),
            P(W, None, "narrow"),
            P(None, NW),
            P(W, None, "narrow"),
            P(None, NW),
            P("narrow", W),
            P(NW),
            P(W, "narrow"),
            P(NW),
            P("narrow", W),
            P(NW),
        ),
        check_vma=False,
    )
```

```python
import jax
import jax.numpy as jnp
from jax import lax
from jax.sharding import Mesh
from jax.sharding import PartitionSpec as P

HEADS = 16


norm_epsilon = 1e-06
gelu_factor = 0.7978845608028654
gelu_cubic = 0.044715


def gelu_tanh(values):
    return (
        0.5
        * values
        * (1.0 + jnp.tanh(gelu_factor * (values + gelu_cubic * values * values * values)))
    )


def gelu_slope(values):
    inner = jnp.tanh(gelu_factor * (values + gelu_cubic * values * values * values))
    return 0.5 * (1.0 + inner) + 0.5 * values * (1.0 - inner * inner) * gelu_factor * (
        1.0 + 3.0 * gelu_cubic * values * values
    )


def norm_forward(values):
    row_mean = jnp.mean(values, axis=1, keepdims=True)
    row_var = jnp.mean(values * values, axis=1, keepdims=True) - row_mean * row_mean
    inverse = lax.rsqrt(row_var + norm_epsilon)
    return (values - row_mean) * inverse, inverse


def norm_backward(grad_normed, normed, inverse):
    mean_one = jnp.mean(grad_normed, axis=1, keepdims=True)
    mean_two = jnp.mean(grad_normed * normed, axis=1, keepdims=True)
    return inverse * (grad_normed - mean_one - normed * mean_two)


def swap_core(values):
    return lax.ppermute(values, "core", [(0, 1), (1, 0)])


def pair_gather(rows):
    other = swap_core(rows)
    mine_first = lax.axis_index("core") == 0
    return jnp.concatenate(
        [jnp.where(mine_first, rows, other), jnp.where(mine_first, other, rows)], axis=0
    )


def pair_scatter(partial):
    half = partial.shape[0] // 2
    core = lax.axis_index("core")
    sent = lax.dynamic_slice_in_dim(partial, (1 - core) * half, half, 0)
    kept = lax.dynamic_slice_in_dim(partial, core * half, half, 0)
    return kept.astype(jnp.float32) + swap_core(sent).astype(jnp.float32)


def shift_narrow(values, step):
    size = lax.axis_size("narrow")
    return lax.ppermute(values, "narrow", [(i, (i + step) % size) for i in range(size)])


def flip_col(values, bit):
    size = lax.axis_size("col")
    return lax.ppermute(values, "col", [(i, i ^ bit) for i in range(size)])


def col_bits():
    bits = []
    bit = 1
    while bit < lax.axis_size("col"):
        bits.append(bit)
        bit *= 2
    return bits


def gather_chips(shard):
    half = shard.shape[0] // 2
    up = shift_narrow(shard, 1)
    down = shift_narrow(shard, -1)
    far = jnp.concatenate([shift_narrow(up[:half], 1), shift_narrow(down[half:], -1)], axis=0)
    line = jnp.stack([shard, up, far, down])
    bits = col_bits()
    sides = []
    for part, order in ((line[:, :half], bits), (line[:, half:], bits[::-1])):
        pieces = {0: part}
        for bit in order:
            for mask in list(pieces):
                pieces[mask | bit] = flip_col(pieces[mask], bit)
        sides.append(jnp.stack([pieces[mask] for mask in range(len(pieces))]))
    return sides


def arrange(sides, low, high):
    col = lax.axis_index("col")
    count = lax.axis_size("col")
    blocks = []
    for side in sides:
        cut = side[..., low:high]
        blocks.append(
            jnp.stack(
                [lax.dynamic_index_in_dim(cut, c ^ col, 0, keepdims=False) for c in range(count)],
                axis=1,
            )
        )
    return jnp.concatenate(blocks, axis=2)


def add_low(left, right):
    return (left.astype(jnp.float32) + right.astype(jnp.float32)).astype(jnp.bfloat16)


def scatter_chips(blocks):
    col = lax.axis_index("col")
    count = lax.axis_size("col")
    half = blocks.shape[2] // 2
    bits = col_bits()
    halves = []
    for part, order in ((blocks[:, :, :half], bits), (blocks[:, :, half:], bits[::-1])):
        pieces = {
            mask: lax.dynamic_index_in_dim(part, mask ^ col, 1, keepdims=False)
            for mask in range(count)
        }
        for bit in order:
            for mask in [m for m in pieces if not m & bit]:
                pieces[mask] = add_low(pieces[mask], flip_col(pieces.pop(mask | bit), bit))
        halves.append(pieces[0])
    line = jnp.concatenate(halves, axis=1)
    own, up, far, down = line[0], line[1], line[2], line[3]
    up_low = add_low(up[:half], shift_narrow(far[:half], -1))
    down_high = add_low(down[half:], shift_narrow(far[half:], 1))
    up_all = jnp.concatenate([up_low, up[half:]], axis=0)
    down_all = jnp.concatenate([down[:half], down_high], axis=0)
    return (
        own.astype(jnp.float32)
        + shift_narrow(up_all, -1).astype(jnp.float32)
        + shift_narrow(down_all, 1).astype(jnp.float32)
    )


def core_rows(values, split_axis, concat_axis):
    return lax.all_to_all(values, "core", split_axis, concat_axis, tiled=True)


def to_images(values, seq_count, half):
    width = values.shape[1]
    shaped = core_rows(values.reshape(seq_count, 2, half, width), 1, 0)
    return lax.all_to_all(
        shaped.reshape(2 * seq_count, half, width), "narrow", 0, 2, tiled=True
    ).reshape(half, -1)


def from_images(values, seq_count):
    half = values.shape[0]
    shaped = lax.all_to_all(values[None], "narrow", 2, 0, tiled=True)
    return core_rows(shaped[:, None], 0, 1).reshape(seq_count * 2 * half, -1)


def per_device(
    tokens,
    condition,
    w_ada,
    b_ada,
    w_qkv,
    b_qv,
    w_proj,
    b_proj,
    w_fc1,
    b_fc1,
    w_fc2,
    b_fc2,
    cotangent,
):
    seq_count = condition.shape[0]
    length = tokens.shape[0] // seq_count
    half = length // 2
    feature_count = condition.shape[1]
    head_dim = feature_count // HEADS
    score_scale = head_dim ** (-0.5)
    narrow = lax.axis_index("narrow")
    col = lax.axis_index("col")
    core = lax.axis_index("core")
    n_size = lax.axis_size("narrow")
    w_size = 2 * lax.axis_size("col")
    wide = 2 * col + core
    part_width = feature_count // 2
    head_count = part_width // head_dim
    unit = feature_count // n_size
    pair = unit // 2
    fc_unit = w_fc1.shape[1]
    fc_half = fc_unit // 2
    rows_low = w_fc1.shape[0]
    rows = 2 * rows_low

    def attend(seq_block):
        outputs = []
        lse_list = []
        for head_index in range(head_count):
            offset = head_index * head_dim
            query_rows = seq_block[0][:, offset : offset + head_dim]
            key_rows = seq_block[1][:, offset : offset + head_dim]
            value_rows = seq_block[2][:, offset : offset + head_dim]
            scores = (
                jnp.einsum("qd,kd->qk", query_rows, key_rows, preferred_element_type=jnp.float32)
                * score_scale
            )
            row_top = jnp.max(scores, axis=1, keepdims=True)
            raised = jnp.exp(scores - row_top)
            row_total = jnp.sum(raised, axis=1, keepdims=True)
            soft_weights = (raised / row_total).astype(jnp.bfloat16)
            outputs.append(jnp.dot(soft_weights, value_rows, preferred_element_type=jnp.float32))
            lse_list.append(row_top[:, 0] + jnp.log(row_total[:, 0]))
        return (jnp.concatenate(outputs, axis=1), jnp.stack(lse_list))

    def attend_back(packed):
        seq_block, lse_rows, grad_block = packed
        pieces = []
        for head_index in range(head_count):
            offset = head_index * head_dim
            query_rows = seq_block[0][:, offset : offset + head_dim]
            key_rows = seq_block[1][:, offset : offset + head_dim]
            value_rows = seq_block[2][:, offset : offset + head_dim]
            grad_head = grad_block[:, offset : offset + head_dim]
            scores = (
                jnp.einsum("qd,kd->qk", query_rows, key_rows, preferred_element_type=jnp.float32)
                * score_scale
            )
            soft_float = jnp.exp(scores - lse_rows[head_index][:, None])
            soft_weights = soft_float.astype(jnp.bfloat16)
            grad_value = jnp.einsum(
                "qk,qd->kd", soft_weights, grad_head, preferred_element_type=jnp.float32
            )
            grad_soft = jnp.einsum(
                "qd,kd->qk", grad_head, value_rows, preferred_element_type=jnp.float32
            )
            inner = jnp.sum(soft_float * grad_soft, axis=1, keepdims=True)
            grad_scores = (soft_float * (grad_soft - inner)).astype(jnp.bfloat16)
            grad_query = (
                jnp.dot(grad_scores, key_rows, preferred_element_type=jnp.float32) * score_scale
            )
            grad_key = (
                jnp.einsum("qk,qd->kd", grad_scores, query_rows, preferred_element_type=jnp.float32)
                * score_scale
            )
            pieces.append([grad_query, grad_key, grad_value])
        return jnp.concatenate(
            [piece[c] for c in range(3) for piece in pieces], axis=1
        ).astype(jnp.bfloat16)


    def turned(values, axis):
        return jnp.take(values, (narrow - jnp.arange(n_size)) % n_size, axis=axis)

    qkv_cut = core_rows(jnp.transpose(w_qkv, (1, 0, 2)), 2, 1)
    proj_cut = core_rows(w_proj, 0, 1).T
    fc1_cut = core_rows(w_fc1, 1, 0)
    fc2_cut = core_rows(w_fc2, 0, 1).T
    pack_one = jnp.concatenate([qkv_cut[0], qkv_cut[1], qkv_cut[2], proj_cut], axis=1)
    sides_one = gather_chips(pack_one)
    pack_two = jnp.concatenate([fc1_cut, fc2_cut], axis=1)
    sides_two = gather_chips(pack_two)

    def matrix(sides, low, high):
        blocks = arrange(sides, low, high)
        return jnp.transpose(blocks, (1, 2, 0, 3)).reshape(feature_count, -1)

    qkv_mats = [matrix(sides_one, c * pair, (c + 1) * pair) for c in range(3)]
    qkv_full = jnp.concatenate(qkv_mats, axis=1)
    proj_full = matrix(sides_one, 3 * pair, 4 * pair)
    fc1_full = matrix(sides_two, 0, fc_half)
    fc2_full = matrix(sides_two, fc_half, 2 * fc_half)

    inputs = to_images(tokens, seq_count, half).astype(jnp.float32)
    small = jnp.concatenate(
        [
            b_ada.reshape(-1),
            b_qv.reshape(-1),
            b_proj,
            b_fc2,
            b_fc1,
            condition.reshape(-1),
        ]
    )
    small = jnp.pad(small, (0, -small.shape[0] % 1024)).reshape(-1, 128)
    smalls = lax.all_gather(small, ("narrow", "col", "core")).reshape(n_size * w_size, -1)
    part = b_proj.shape[0]

    def full_bias(low, count):
        return jnp.transpose(
            smalls[:, low : low + count * part].reshape(n_size * w_size, count, part), (1, 0, 2)
        ).reshape(count, feature_count)

    ada_bias = full_bias(0, 6).astype(jnp.float32)
    qv_bias = full_bias(6 * part, 2)
    proj_bias = full_bias(8 * part, 1).astype(jnp.float32)
    fc2_bias = full_bias(9 * part, 1).astype(jnp.float32)
    fc1_size = b_fc1.shape[0]
    fc1_rows = smalls[:, 10 * part : 10 * part + fc1_size].reshape(n_size, 2, fc_half)
    fc1_bias = turned(lax.dynamic_index_in_dim(fc1_rows, core, 1, keepdims=False), 0)
    fc1_bias = fc1_bias.reshape(1, -1).astype(jnp.float32)
    qv_rows = lax.dynamic_index_in_dim(
        qv_bias.reshape(2, n_size, 2, pair), core, 2, keepdims=False
    )
    qv_rows = turned(qv_rows, 1).reshape(2, -1).astype(jnp.float32)
    qkv_bias = jnp.concatenate([qv_rows[0], jnp.zeros_like(qv_rows[0]), qv_rows[1]])

    cond_all = smalls[
        :w_size, 10 * part + fc1_size : 10 * part + fc1_size + condition.size
    ].reshape(-1, feature_count)
    cond_act_all = jax.nn.silu(cond_all.astype(jnp.float32)).astype(jnp.bfloat16)
    cond_cols = lax.dynamic_slice_in_dim(cond_act_all, wide * rows_low, rows_low, 1)
    mod_part = jnp.einsum("sd,dcn->scn", cond_cols, w_ada, preferred_element_type=jnp.float32)
    mod_total = lax.psum(mod_part, ("col", "core"))
    mod_rows = lax.dynamic_slice_in_dim(mod_total, col * n_size, n_size, 0)
    modulation = lax.all_to_all(mod_rows, "narrow", 0, 2, tiled=True).reshape(6, -1) + ada_bias
    shift_one, scale_one, gate_one, shift_two, scale_two, gate_two = [
        modulation[i : i + 1] for i in range(6)
    ]

    normed_one, inverse_one = norm_forward(inputs)
    hidden_one = (normed_one * (1.0 + scale_one) + shift_one).astype(jnp.bfloat16)
    hidden_one_full = pair_gather(hidden_one)
    qkv_low = (
        jnp.dot(hidden_one_full, qkv_full, preferred_element_type=jnp.float32) + qkv_bias
    ).astype(jnp.bfloat16)
    qkv_parts = [qkv_low[:, c * part_width : (c + 1) * part_width] for c in range(3)]
    attended, lse_rows = attend(qkv_parts)
    attended_low = attended.astype(jnp.bfloat16)
    attn_branch = (
        pair_scatter(
            jnp.einsum(
                "th,dh->td", attended_low, proj_full, preferred_element_type=jnp.float32
            ).astype(jnp.bfloat16)
        )
        + proj_bias
    )
    residual = inputs + attn_branch * gate_one
    normed_two, inverse_two = norm_forward(residual)
    hidden_two = (normed_two * (1.0 + scale_two) + shift_two).astype(jnp.bfloat16)
    hidden_two_full = pair_gather(hidden_two)
    grad_out = to_images(cotangent, seq_count, half).astype(jnp.float32)
    grad_mlp = (grad_out * gate_two).astype(jnp.bfloat16)
    grad_mlp_full = pair_gather(grad_mlp)
    pre_act = jnp.dot(hidden_two_full, fc1_full, preferred_element_type=jnp.float32) + fc1_bias
    activated = gelu_tanh(pre_act).astype(jnp.bfloat16)
    grad_act = jnp.dot(grad_mlp_full, fc2_full, preferred_element_type=jnp.float32)
    grad_pre = (grad_act * gelu_slope(pre_act)).astype(jnp.bfloat16)

    def blocked(grad):
        return jnp.transpose(
            grad.astype(jnp.bfloat16).reshape(-1, rows, n_size, grad.shape[1] // n_size),
            (2, 0, 1, 3),
        )

    grad_fc1_part = jnp.einsum(
        "td,tf->df", hidden_two_full, grad_pre, preferred_element_type=jnp.float32
    )
    grad_fc2_part = jnp.einsum(
        "td,tf->df", grad_mlp_full, activated, preferred_element_type=jnp.float32
    )
    total_fc1 = scatter_chips(blocked(grad_fc1_part))
    total_fc2 = scatter_chips(blocked(grad_fc2_part))
    grad_hidden_two = pair_scatter(
        jnp.einsum("tf,df->td", grad_pre, fc1_full, preferred_element_type=jnp.float32).astype(
            jnp.bfloat16
        )
    )
    mlp_branch = (
        pair_scatter(
            jnp.einsum(
                "tf,df->td", activated, fc2_full, preferred_element_type=jnp.float32
            ).astype(jnp.bfloat16)
        )
        + fc2_bias
    )
    output = from_images((residual + mlp_branch * gate_two).astype(jnp.bfloat16), seq_count)

    grad_residual = grad_out + norm_backward(
        grad_hidden_two * (1.0 + scale_two), normed_two, inverse_two
    )
    grad_attn = (grad_residual * gate_one).astype(jnp.bfloat16)
    grad_attn_full = pair_gather(grad_attn)
    grad_proj_part = jnp.einsum(
        "td,th->dh", grad_attn_full, attended_low, preferred_element_type=jnp.float32
    )
    grad_attended = jnp.dot(
        grad_attn_full, proj_full, preferred_element_type=jnp.float32
    ).astype(jnp.bfloat16)
    grad_qkv = attend_back((qkv_parts, lse_rows, grad_attended))
    grad_hidden_one = pair_scatter(
        jnp.einsum("tn,dn->td", grad_qkv, qkv_full, preferred_element_type=jnp.float32).astype(
            jnp.bfloat16
        )
    )
    grad_qkv_part = jnp.einsum(
        "td,tn->dn", hidden_one_full, grad_qkv, preferred_element_type=jnp.float32
    )
    grad_inputs = grad_residual + norm_backward(
        grad_hidden_one * (1.0 + scale_one), normed_one, inverse_one
    )
    grad_tokens = from_images(grad_inputs.astype(jnp.bfloat16), seq_count).astype(jnp.float32)
    total_one = scatter_chips(
        jnp.concatenate(
            [blocked(grad_qkv_part[:, c * part_width : (c + 1) * part_width]) for c in range(3)]
            + [blocked(grad_proj_part)],
            axis=3,
        )
    )

    def sums(values):
        return jnp.sum(values.astype(jnp.float32), axis=0)

    packed = jnp.concatenate(
        [
            sums(grad_hidden_one),
            sums(grad_hidden_one * normed_one),
            sums(grad_residual * attn_branch),
            sums(grad_hidden_two),
            sums(grad_hidden_two * normed_two),
            sums(grad_out * mlp_branch),
            sums(grad_mlp),
            sums(grad_attn),
            turned(sums(grad_pre).reshape(n_size, fc_half), 0).reshape(-1),
            turned(sums(grad_qkv[:, :part_width]).reshape(n_size, pair), 0).reshape(-1),
            turned(sums(grad_qkv[:, 2 * part_width :]).reshape(n_size, pair), 0).reshape(-1),
        ]
    )
    packs = lax.all_gather(packed, ("col", "narrow", "core"))
    packs = packs.reshape(-1, 2, packed.shape[0])
    d = feature_count
    grad_mod = jnp.sum(packs[:, :, : 6 * d], axis=1).astype(jnp.bfloat16).reshape(-1, 6, d)
    cores = jnp.sum(packs[:, :, 6 * d :], axis=0)
    both = jnp.sum(cores[:, : 2 * d], axis=0)
    place = narrow * w_size + wide
    grad_b_fc2 = lax.dynamic_slice_in_dim(both[:d], place * part, part, 0)
    grad_b_proj = lax.dynamic_slice_in_dim(both[d:], place * part, part, 0)
    fc1_sums = jnp.transpose(
        cores[:, 2 * d : 2 * d + n_size * fc_half].reshape(2, n_size, fc_half), (1, 0, 2)
    ).reshape(-1)
    grad_b_fc1 = lax.dynamic_slice_in_dim(fc1_sums, place * fc1_size, fc1_size, 0)
    qv_sums = jnp.transpose(
        cores[:, 2 * d + n_size * fc_half :].reshape(2, 2, n_size, pair), (1, 2, 0, 3)
    ).reshape(2, d)
    grad_b_qv = lax.dynamic_slice_in_dim(qv_sums, place * part, part, 1)
    ada_sums = jnp.sum(grad_mod.astype(jnp.float32), axis=0)
    grad_b_ada = lax.dynamic_slice_in_dim(ada_sums, place * part, part, 1)
    mod_slice = lax.dynamic_slice_in_dim(grad_mod, narrow * unit, unit, 2)
    grad_w_ada = jnp.einsum(
        "sd,scn->dcn", cond_cols, mod_slice, preferred_element_type=jnp.float32
    )
    cond_part = jnp.einsum("scn,dcn->sd", mod_slice, w_ada, preferred_element_type=jnp.float32)
    cond_parts = lax.all_gather(cond_part, ("narrow", "col", "core"))
    cond_rows = lax.dynamic_slice_in_dim(cond_parts, wide * seq_count, seq_count, 1)
    cond_sum = jnp.sum(cond_rows.reshape(n_size, w_size, seq_count, rows_low), axis=0)
    cond_total = jnp.transpose(cond_sum, (1, 0, 2)).reshape(seq_count, d)
    cond_float = condition.astype(jnp.float32)
    sigmoid_cond = jax.nn.sigmoid(cond_float)
    grad_cond = cond_total * sigmoid_cond * (1.0 + cond_float * (1.0 - sigmoid_cond))

    low_one = total_one.astype(jnp.bfloat16)
    qkv_out = jnp.stack([low_one[:, c * pair : (c + 1) * pair] for c in range(3)])
    grad_w_qkv = jnp.transpose(core_rows(qkv_out, 1, 2).astype(jnp.float32), (1, 0, 2))
    grad_w_proj = core_rows(low_one[:, 3 * pair :].T, 1, 0).astype(jnp.float32)
    grad_w_fc1 = core_rows(total_fc1.astype(jnp.bfloat16), 0, 1).astype(jnp.float32)
    grad_w_fc2 = core_rows(total_fc2.astype(jnp.bfloat16).T, 1, 0).astype(jnp.float32)
    return (
        output,
        grad_tokens,
        grad_cond,
        grad_w_ada,
        grad_b_ada,
        grad_w_qkv,
        grad_b_qv,
        grad_w_proj,
        grad_b_proj,
        grad_w_fc1,
        grad_b_fc1,
        grad_w_fc2,
        grad_b_fc2,
    )


W = ("col", "core")
NW = ("narrow", "col", "core")


def solution(mesh):
    devices = mesh.devices
    split = Mesh(devices.reshape(devices.shape[0], devices.shape[1] // 2, 2), NW)
    return jax.shard_map(
        per_device,
        mesh=split,
        in_specs=(
            P(W, "narrow"),
            P(W, None),
            P(W, None, "narrow"),
            P(None, NW),
            P(W, None, "narrow"),
            P(None, NW),
            P("narrow", W),
            P(NW),
            P(W, "narrow"),
            P(NW),
            P("narrow", W),
            P(NW),
            P(W, "narrow"),
        ),
        out_specs=(
            P(W, "narrow"),
            P(W, "narrow"),
            P(W, None),
            P(W, None, "narrow"),
            P(None, NW),
            P(W, None, "narrow"),
            P(None, NW),
            P("narrow", W),
            P(NW),
            P(W, "narrow"),
            P(NW),
            P("narrow", W),
            P(NW),
        ),
        check_vma=False,
    )
```
